32 devices in a mesh: wide: 8 (over z, y), slab: 4 (over x, core).
Axes of the slice: x: 2, y: 2, z: 4, core: 2. Of those that a mesh axis runs over, the one named last changes fastest.
Arguments:
- thermal_state: float32 [8, 64, 32, 1024], P('wide', 'slab'), may hold values from -5 to 5
- thermal_spreading_rate: bfloat16 [8, 64, 32, 1024], P('wide', 'slab'), may hold values from 0.5 to 1.5
- flow_speed_vector: bfloat16 [3, 8, 64, 32, 1024], P(None, 'wide', 'slab'), may hold values from -0.796875 to 0.796875
- interface_guess: float32 [8, 1024], P('wide', 'slab'), may hold values from -4 to 4
- partner_facing_rows: int32 [8, 1024], P('wide', 'slab'), may hold values from 0 to 1023, each once within a row
- mismatch_change_matrix: float32 [8, 1024, 128], P('wide', 'slab'), may hold values from -5 to 5
- output_change_matrix: float32 [8, 1024, 128], P('wide', 'slab'), may hold values from -1.8 to 1.8
Outputs:
- temperature_out: float32 [8, 64, 32, 1024], P('wide', 'slab')
- updated_interface_guess: float32 [8, 1024], P('wide', 'slab')
- unitary_basis_factor: float32 [8, 1024, 128], P('wide', 'slab')
The draws below stay inside these ranges and needn't reach their ends.
Inputs may be any that keep to these rules, and one draw needn't show every extreme that they name: `partner_facing_rows`: each partition's rows of matching are a permutation of its partner's interface rows.
All inputs are finite; a program needn't handle non-finite values.
Results may differ from the reference program's by a relative error of at most 0.0003.
Values may be sent and summed in bfloat16 or wider, within the bound.
A program may use at most 64 MiB of HBM per device.

```python
import jax
import jax.numpy as jnp
from jax import lax

GRID_SPAN_TWO = 32
GRID_SPAN_DEPTH = 1024
INTERFACE_STRIP = 64
COLS = 128
SWEEPS = 4
GRID_SPAN_ONE = 64
IFACE = 1024
N_WIDE = 8


def draw_mismatch_change_matrix(key, part):
    first_key, second_key, third_key = jax.random.split(key, 3)
    array_dimensions = (N_WIDE, IFACE, COLS)
    normal_part = jnp.clip(jax.random.normal(first_key, array_dimensions, jnp.float32), -5.0, 5.0)
    row_scales = 10.0 ** jax.random.uniform(second_key, (N_WIDE, IFACE, 1), jnp.float32)
    column_scales = 10.0 ** jax.random.uniform(third_key, (1, 1, COLS), jnp.float32)
    position = (jnp.arange(N_WIDE, dtype=jnp.float32)[:, None] * IFACE + jnp.arange(IFACE, dtype=jnp.float32)[None, :]) / (N_WIDE * IFACE)
    rising = 1.0 + 2.0 * position[:, :, None]
    return 0.0005 * normal_part * row_scales * column_scales * rising


def level_of(rng, shape, cuts, least, largest):
    level, own = 1.0, jax.random.fold_in(rng, 6)
    for dim, blocks in cuts:
        heights = jnp.exp(jax.random.uniform(jax.random.fold_in(own, dim), (blocks,), jnp.float32, least / len(cuts), largest / len(cuts)))
        level = level * jnp.repeat(heights, shape[dim] // blocks).reshape([-1 if axis == dim else 1 for axis in range(len(shape))])
    return level


def scatter_about(key, shape, scale, most, shards=(), held_as=jnp.bfloat16):
    gain = level_of(key, shape, shards, -0.22, 0.18) if shards else 1.0
    drawn = jax.random.normal(key, shape, jnp.float32) * scale * gain
    return jnp.minimum(jnp.maximum(drawn, -most), most).astype(held_as)


def setup_inputs(seed: int = 0) -> dict:
    splits = jax.random.split(jax.random.key(seed), 8)
    return {
        "thermal_state": scatter_about(splits[0], (N_WIDE, GRID_SPAN_ONE, GRID_SPAN_TWO, GRID_SPAN_DEPTH), 1.0, 5.0, ((0, 8), (1, 4)), jnp.float32),
        "thermal_spreading_rate": jnp.clip(0.5 + 1.0 * jax.random.uniform(splits[1], (N_WIDE, GRID_SPAN_ONE, GRID_SPAN_TWO, GRID_SPAN_DEPTH), jnp.float32) ** level_of(splits[1], (N_WIDE, GRID_SPAN_ONE, GRID_SPAN_TWO, GRID_SPAN_DEPTH), ((0, 8), (1, 4)), -0.2, 0.2), 0.5, 1.5).astype(jnp.bfloat16),
        "flow_speed_vector": jnp.clip(jax.random.uniform(splits[2], (3, N_WIDE, GRID_SPAN_ONE, GRID_SPAN_TWO, GRID_SPAN_DEPTH), jnp.float32, -0.796875, 0.796875) * level_of(splits[2], (3, N_WIDE, GRID_SPAN_ONE, GRID_SPAN_TWO, GRID_SPAN_DEPTH), ((1, 8), (2, 4)), -0.4, 0.0), -0.796875, 0.796875).astype(jnp.bfloat16),
        "interface_guess": scatter_about(splits[3], (N_WIDE, IFACE), 1.0, 4.0, ((0, 8), (1, 4)), jnp.float32),
        "partner_facing_rows": jax.vmap(lambda own: jax.random.permutation(own, IFACE))(jax.random.split(splits[4], N_WIDE)).reshape((N_WIDE, IFACE)).astype(jnp.int32),
        "mismatch_change_matrix": draw_mismatch_change_matrix(jax.random.fold_in(splits[7], 71), 0),
        "output_change_matrix": scatter_about(splits[6], (N_WIDE, IFACE, COLS), 0.3, 1.8, ((0, 8), (1, 4)), jnp.float32),
    }


STEP_SIZE = 0.11

def surround_wrapper(block_rows, mirror_layer):
    bottom = jnp.zeros((block_rows.shape[0], 1, block_rows.shape[2]), block_rows.dtype)
    stacked = jnp.concatenate([bottom, block_rows, mirror_layer[:, None, :]], axis=1)
    return jnp.pad(stacked, ((0, 0), (0, 0), (1, 1)))

def march_forward(bordered_array, diffuse_subdomain, subdomain_flow_speed):
    centre = bordered_array[1:-1, 1:-1, 1:-1]
    plus_first = bordered_array[2:, 1:-1, 1:-1]
    minus_first = bordered_array[:-2, 1:-1, 1:-1]
    plus_second = bordered_array[1:-1, 2:, 1:-1]
    minus_second = bordered_array[1:-1, :-2, 1:-1]
    plus_third = bordered_array[1:-1, 1:-1, 2:]
    minus_third = bordered_array[1:-1, 1:-1, :-2]
    spread = plus_first + minus_first + plus_second + minus_second + plus_third + minus_third - 6.0 * centre
    carried = 0.5 * (subdomain_flow_speed[0].astype(jnp.float32) * (plus_first - minus_first) + subdomain_flow_speed[1].astype(jnp.float32) * (plus_second - minus_second) + subdomain_flow_speed[2].astype(jnp.float32) * (plus_third - minus_third))
    return centre + STEP_SIZE * (diffuse_subdomain.astype(jnp.float32) * spread - carried)

def reference(thermal_state, thermal_spreading_rate, flow_speed_vector, interface_guess, partner_facing_rows, mismatch_change_matrix, output_change_matrix):
    ghost_all = jnp.repeat(interface_guess.reshape(N_WIDE, GRID_SPAN_ONE, GRID_SPAN_DEPTH // INTERFACE_STRIP), INTERFACE_STRIP, axis=2)

    def evolve(voxel_position):
        subdomain_thermal_state = thermal_state[voxel_position]
        diffuse_subdomain = thermal_spreading_rate[voxel_position]
        subdomain_flow_speed = flow_speed_vector[:, voxel_position]
        mirror_layer = jnp.pad(ghost_all[voxel_position], ((1, 1), (0, 0)))
        for sweep in range(SWEEPS):
            bordered_array = surround_wrapper(jnp.pad(subdomain_thermal_state, ((1, 1), (0, 0), (0, 0))), mirror_layer)
            subdomain_thermal_state = march_forward(bordered_array, diffuse_subdomain, subdomain_flow_speed)
        return subdomain_thermal_state
    final = lax.map(evolve, jnp.arange(N_WIDE))
    face_means = lax.optimization_barrier(jnp.mean(final[:, :, GRID_SPAN_TWO - 1, :].reshape(N_WIDE, GRID_SPAN_ONE, GRID_SPAN_DEPTH // INTERFACE_STRIP, INTERFACE_STRIP), axis=3))
    face_means = face_means.reshape(N_WIDE, IFACE)
    partner = jnp.roll(face_means, N_WIDE // 2, axis=0)
    tilde = jnp.take_along_axis(partner, partner_facing_rows, axis=1)
    resid = tilde - interface_guess
    flat = mismatch_change_matrix.reshape(N_WIDE * IFACE, COLS)
    gram_matrix = lax.dot_general(flat.astype(jnp.float32), flat.astype(jnp.float32), (((0,), (0,)), ((), ())), precision=lax.Precision.HIGHEST, preferred_element_type=jnp.float32)
    projection = jnp.dot(resid.reshape(N_WIDE * IFACE).astype(jnp.float32), flat.astype(jnp.float32), precision=lax.Precision.HIGHEST, preferred_element_type=jnp.float32)
    lower_factor = jnp.linalg.cholesky(gram_matrix)
    half_solve = lax.linalg.triangular_solve(lower_factor, projection[:, None], left_side=True, lower=True)
    coefficients = -lax.linalg.triangular_solve(lower_factor, half_solve, left_side=True, lower=True, transpose_a=True)[:, 0]
    update = jnp.dot(output_change_matrix.reshape(N_WIDE * IFACE, COLS).astype(jnp.float32), coefficients.astype(jnp.float32), precision=lax.Precision.HIGHEST, preferred_element_type=jnp.float32)
    updated_interface_guess = tilde + update.reshape(N_WIDE, IFACE)
    scaled = lax.linalg.triangular_solve(lower_factor, flat, left_side=False, lower=True, transpose_a=True)
    unitary_basis_factor = (jnp.sqrt(jnp.float32(N_WIDE * IFACE)) * scaled).reshape(N_WIDE, IFACE, COLS)
    return (final, updated_interface_guess, unitary_basis_factor)
```

```python
import functools
import math

import jax
import jax.numpy as jnp
from jax import lax
from jax.experimental import pallas as pl
from jax.experimental.pallas import tpu as pltpu
from jax.sharding import PartitionSpec as P

INTERFACE_STRIP = 64
SWEEPS = 4
STEP_SIZE = 0.11
TOP = 8
MESH = pl.DeviceIdType.MESH
HIGHEST = lax.Precision.HIGHEST
F32 = jnp.float32
BF16 = jnp.bfloat16


def iota(shape, dim):
    return lax.broadcasted_iota(jnp.int32, shape, dim)


def split3(value):
    hi = value.astype(BF16).astype(F32)
    rest = value - hi
    mid = rest.astype(BF16).astype(F32)
    return hi, mid, rest - mid


def march_rows(centre, plus_first, minus_first, plus_second, minus_second, rate, flow):
    depth = centre.shape[1]
    lane = iota((centre.shape[0], 128), 1)
    right = pltpu.roll(centre, depth - 1, 1)
    left = pltpu.roll(centre, 1, 1)
    plus_third = jnp.concatenate(
        [right[:, : depth - 128], jnp.where(lane == 127, 0.0, right[:, depth - 128 :])], axis=1
    )
    minus_third = jnp.concatenate(
        [jnp.where(lane == 0, 0.0, left[:, :128]), left[:, 128:]], axis=1
    )
    spread = (
        (plus_first + minus_first)
        + (plus_second + minus_second)
        + (plus_third + minus_third)
        - 6.0 * centre
    )
    carried = (
        flow[0].astype(F32) * (plus_first - minus_first)
        + flow[1].astype(F32) * (plus_second - minus_second)
        + flow[2].astype(F32) * (plus_third - minus_third)
    )
    return centre + (STEP_SIZE * rate.astype(F32) * spread - (0.5 * STEP_SIZE) * carried)


def eliminate(strips, first, last, blocks):
    lane = iota((8, 128), 1)
    row = iota((8, 128), 0)

    def block(b, strips):
        strips = list(strips)
        for i in range(8):
            columns = [jnp.broadcast_to(s[:, i : i + 1], (8, 128)) for s in strips]
            pivot = jnp.broadcast_to(columns[0][i : i + 1, :], (8, 128))
            inverse = 1.0 / pivot
            along = jnp.broadcast_to(strips[0][i : i + 1, :], (8, 128))
            scaled = jnp.where(lane == i, inverse, along * inverse)
            below = row > i
            strips[0] = jnp.where((lane == i) & below, 0.0, strips[0]) - jnp.where(
                below, columns[0], 0.0
            ) * scaled
            for t in range(1, blocks):
                strips[t] = jnp.where(lane == i, 0.0, strips[t]) - columns[t] * scaled
        kept = ((lane < 8) & (lane <= row)) | (lane >= 8 * (blocks - b))
        strips[0] = jnp.where(kept, strips[0], 0.0)
        strips = [pltpu.roll(s, 128 - 8, 1) for s in strips]
        return tuple(strips[1:] + strips[:1])

    return lax.fori_loop(first, last, block, tuple(strips))


def kernel(
    n_wide,
    n_slab,
    total_rows,
    state_hbm,
    rate_hbm,
    flow_hbm,
    guess_ref,
    rows_ref,
    panel_ref,
    output_ref,
    final_hbm,
    updated_ref,
    basis_ref,
    cells,
    halo,
    rate,
    flow,
    spread_map,
    pick_map,
    gram_own,
    gram_scatter,
    gram_sum,
    gram_wide,
    gram_part,
    gram_full,
    elim,
    face_own,
    face_all,
    proj_own,
    proj_slab,
    proj_sum,
    proj_wide,
    load_sem,
    store_sem,
    halo_send,
    halo_recv,
    slab_send,
    slab_recv,
    wide_send,
    wide_recv,
    face_send,
    face_recv,
):
    layers, depth = cells.shape[1], cells.shape[3]
    height = rate.shape[1]
    cols = panel_ref.shape[1]
    rows_dev = guess_ref.shape[1]
    per_layer = depth // INTERFACE_STRIP
    part_rows = cols // n_slab
    me_w, me_s = lax.axis_index("wide"), lax.axis_index("slab")
    across = lax.rem(me_w + n_wide // 2, n_wide)

    def slab_peer(k):
        return lax.rem(me_s + k, n_slab)

    def wide_peer(k):
        return lax.rem(me_w + k, n_wide)

    quarter = layers // 4
    loads = {}
    for g in (0, 3, 1, 2):
        planes = pl.ds(g * quarter, quarter)
        loads[g] = [
            pltpu.make_async_copy(
                state_hbm.at[0, planes], cells.at[0, planes, pl.ds(TOP, height)], load_sem.at[g, 0]
            ),
            pltpu.make_async_copy(rate_hbm.at[0, planes], rate.at[planes], load_sem.at[g, 1]),
            pltpu.make_async_copy(
                flow_hbm.at[:, 0, planes], flow.at[:, planes], load_sem.at[g, 2]
            ),
        ]
        for c in loads[g]:
            c.start()

    zeros = jnp.zeros((height, depth), F32)
    for side in range(2):

        @pl.when(me_s == side * (n_slab - 1))
        def _():
            for sweep in range(SWEEPS):
                halo[sweep, side] = zeros

    barrier = pltpu.get_barrier_semaphore()
    peers = (
        [(me_w, slab_peer(k)) for k in range(1, n_slab)]
        + [(wide_peer(k), me_s) for k in range(1, n_wide)]
        + [(across, slab_peer(k)) for k in range(1, n_slab)]
    )
    for peer in peers:
        pl.semaphore_signal(barrier, inc=1, device_id=peer, device_id_type=MESH)
    pl.semaphore_wait(barrier, len(peers))

    def halo_copies(sweep, low, high):
        down = pltpu.make_async_remote_copy(
            src_ref=low,
            dst_ref=halo.at[sweep, 1],
            send_sem=halo_send.at[sweep, 0],
            recv_sem=halo_recv.at[sweep, 1],
            device_id=(me_w, lax.max(me_s - 1, 0)),
            device_id_type=MESH,
        )
        up = pltpu.make_async_remote_copy(
            src_ref=high,
            dst_ref=halo.at[sweep, 0],
            send_sem=halo_send.at[sweep, 1],
            recv_sem=halo_recv.at[sweep, 0],
            device_id=(me_w, lax.min(me_s + 1, n_slab - 1)),
            device_id_type=MESH,
        )
        return down, up

    def send_halo(copies):
        @pl.when(me_s > 0)
        def _():
            copies[0].start()

        @pl.when(me_s < n_slab - 1)
        def _():
            copies[1].start()

    def wait_halo(copies):
        @pl.when(me_s > 0)
        def _():
            copies[0].wait_send()
            copies[1].wait_recv()

        @pl.when(me_s < n_slab - 1)
        def _():
            copies[1].wait_send()
            copies[0].wait_recv()

    copies = halo_copies(0, state_hbm.at[0, 0], state_hbm.at[0, layers - 1])
    send_halo(copies)

    def slab_exchange(source, target, phase):
        out = []
        for k in range(1, n_slab):
            c = pltpu.make_async_remote_copy(
                src_ref=source(slab_peer(k)),
                dst_ref=target.at[me_s],
                send_sem=slab_send.at[phase, k],
                recv_sem=slab_recv.at[phase, k],
                device_id=(me_w, slab_peer(k)),
                device_id_type=MESH,
            )
            c.start()
            out.append(c)
        return out

    def wide_exchange(source, target, phase):
        out = []
        for k in range(1, n_wide):
            c = pltpu.make_async_remote_copy(
                src_ref=source,
                dst_ref=target.at[me_w],
                send_sem=wide_send.at[phase, k],
                recv_sem=wide_recv.at[phase, k],
                device_id=(wide_peer(k), me_s),
                device_id_type=MESH,
            )
            c.start()
            out.append(c)
        return out

    def finish(exchange):
        for c in exchange:
            c.wait()

    def summed(ref, count):
        total = ref[0]
        for k in range(1, count):
            total = total + ref[k]
        return total

    panel = panel_ref[...]
    gram = lax.dot_general(
        panel, panel, (((0,), (0,)), ((), ())), precision=HIGHEST, preferred_element_type=F32
    )
    gram_own[...] = gram.reshape(n_slab, part_rows, cols)
    exchange = slab_exchange(lambda peer: gram_own.at[peer], gram_scatter, 0)
    gram_scatter[me_s] = gram_own[me_s]

    line = iota((rows_dev, depth), 0)
    strip = iota((rows_dev, depth), 1) // INTERFACE_STRIP
    spread_map[...] = jnp.where(lax.rem(line, per_layer) == strip, 1.0, 0.0).astype(BF16)
    owner = iota((layers, rows_dev), 1) // per_layer == iota((layers, rows_dev), 0)
    guess = guess_ref[...]
    placed = jnp.where(owner, jnp.broadcast_to(guess, (layers, rows_dev)), 0.0)
    ghost = jnp.zeros((layers, depth), F32)
    for piece in split3(placed):
        ghost = ghost + jnp.dot(piece.astype(BF16), spread_map[...], preferred_element_type=F32)
    empty = jnp.zeros((1, depth), F32)
    for side in range(2):
        for x in range(layers):
            cells[side, x, TOP + height : TOP + height + 1, :] = ghost[x : x + 1, :]
            cells[side, x, TOP - 1 : TOP, :] = empty

    def march_plane(now, x, below, above):
        for y in range(0, height, 16):
            cells[1 - now, x, TOP + y : TOP + y + 16, :] = march_rows(
                cells[now, x, TOP + y : TOP + y + 16, :],
                above(y),
                below(y),
                cells[now, x, TOP + y + 1 : TOP + y + 17, :],
                cells[now, x, TOP + y - 1 : TOP + y + 15, :],
                rate[x, y : y + 16, :],
                [flow[d, x, y : y + 16, :] for d in range(3)],
            )

    def plane_of(now, x):
        return lambda y: cells[now, x, TOP + y : TOP + y + 16, :]

    def halo_of(sweep, side):
        return lambda y: halo[sweep, side, y : y + 16, :]

    for g in (0, 3):
        for c in loads[g]:
            c.wait()
    for sweep in range(SWEEPS):
        now = sweep % 2
        wait_halo(copies)
        march_plane(now, 0, halo_of(sweep, 0), plane_of(now, 1))
        march_plane(now, layers - 1, plane_of(now, layers - 2), halo_of(sweep, 1))
        if sweep < SWEEPS - 1:
            copies = halo_copies(
                sweep + 1,
                cells.at[1 - now, 0, pl.ds(TOP, height)],
                cells.at[1 - now, layers - 1, pl.ds(TOP, height)],
            )
            send_halo(copies)
        if sweep == 0:
            for g in (1, 2):
                for c in loads[g]:
                    c.wait()

        def interior(x, _):
            march_plane(now, x, plane_of(now, x - 1), plane_of(now, x + 1))
            return 0

        lax.fori_loop(1, layers - 1, interior, 0)
        if sweep == 0:
            finish(exchange)
            gram_sum[...] = summed(gram_scatter, n_slab)
            gram_wide[me_w] = gram_sum[...]
            exchange = wide_exchange(gram_sum, gram_wide, 0)
        elif sweep == 1:
            finish(exchange)
            gram_part[...] = summed(gram_wide, n_wide)
            gram_full[me_s] = gram_part[...]
            exchange = slab_exchange(lambda peer: gram_part, gram_full, 1)

    last = SWEEPS % 2
    store = pltpu.make_async_copy(
        cells.at[last, :, pl.ds(TOP, height)], final_hbm.at[0], store_sem
    )
    store.start()

    face_cells = jnp.concatenate(
        [cells[last, x, TOP + height - 1 : TOP + height, :] for x in range(layers)], axis=0
    )
    sums = jnp.zeros((layers, rows_dev), F32)
    for piece in split3(face_cells):
        sums = sums + lax.dot_general(
            piece.astype(BF16),
            spread_map[...],
            (((1,), (1,)), ((), ())),
            preferred_element_type=F32,
        )
    means = jnp.sum(jnp.where(owner, sums, 0.0), axis=0, keepdims=True) * (1.0 / INTERFACE_STRIP)
    face_own[...] = jnp.broadcast_to(means, (8, rows_dev))
    faces = []
    for k in range(n_slab):
        c = pltpu.make_async_remote_copy(
            src_ref=face_own,
            dst_ref=face_all.at[me_s],
            send_sem=face_send.at[k],
            recv_sem=face_recv.at[k],
            device_id=(across, slab_peer(k)),
            device_id_type=MESH,
        )
        c.start()
        faces.append(c)

    facing = rows_ref[...]
    for s in range(n_slab):
        picked = iota((rows_dev, rows_dev), 0) + s * rows_dev == jnp.broadcast_to(
            facing, (rows_dev, rows_dev)
        )
        pick_map[s] = jnp.where(picked, 1.0, 0.0).astype(BF16)

    finish(exchange)
    blocks = cols // 8
    square = gram_full[...].reshape(cols, cols)
    strips = [square[8 * t : 8 * t + 8, :] for t in range(blocks)]
    third = blocks // 3
    strips = eliminate(strips, 0, third, blocks)

    finish(faces)
    line8 = iota((8, rows_dev), 0)
    tilde = jnp.zeros((8, rows_dev), F32)
    for s in range(n_slab):
        hi, mid, low = split3(face_all[s])
        triple = jnp.where(line8 == 0, hi, jnp.where(line8 == 1, mid, low))
        triple = jnp.where(line8 < 3, triple, 0.0).astype(BF16)
        tilde = tilde + jnp.dot(triple, pick_map[s], preferred_element_type=F32)
    tilde = jnp.sum(tilde, axis=0, keepdims=True)
    resid = tilde - guess
    proj_own[...] = jnp.dot(
        jnp.broadcast_to(resid, (8, rows_dev)),
        panel_ref[...],
        precision=HIGHEST,
        preferred_element_type=F32,
    )
    proj_slab[me_s] = proj_own[...]
    exchange = slab_exchange(lambda peer: proj_own, proj_slab, 2)
    strips = eliminate(strips, third, 2 * third, blocks)
    finish(exchange)
    proj_sum[...] = summed(proj_slab, n_slab)
    proj_wide[me_w] = proj_sum[...]
    exchange = wide_exchange(proj_sum, proj_wide, 1)
    strips = eliminate(strips, 2 * third, blocks, blocks)

    for t in range(blocks):
        on_diagonal = iota((8, cols), 1) == iota((8, cols), 0) + 8 * t
        pivots = jnp.sum(jnp.where(on_diagonal, strips[t], 0.0), axis=1, keepdims=True)
        root = 1.0 / jnp.sqrt(jnp.broadcast_to(pivots, (8, cols)))
        elim[8 * t : 8 * t + 8, :] = jnp.where(on_diagonal, 1.0, strips[t]) * root
    inverse = elim[...]
    basis_ref[...] = math.sqrt(total_rows) * lax.dot_general(
        panel_ref[...],
        inverse,
        (((1,), (1,)), ((), ())),
        precision=HIGHEST,
        preferred_element_type=F32,
    )
    finish(exchange)
    projection = summed(proj_wide, n_wide)
    half = lax.dot_general(
        projection,
        inverse,
        (((1,), (1,)), ((), ())),
        precision=HIGHEST,
        preferred_element_type=F32,
    )
    coefficients = jnp.dot(half, inverse, precision=HIGHEST, preferred_element_type=F32)
    update = lax.dot_general(
        coefficients,
        output_ref[...],
        (((1,), (1,)), ((), ())),
        precision=HIGHEST,
        preferred_element_type=F32,
    )
    updated_ref[...] = tilde - update[:1, :]
    store.wait()


def shards(n_wide, n_slab, state, rate, flow, guess, rows, panel, output):
    _, layers, height, depth = state.shape
    rows_dev, cols = panel.shape[1:]
    part_rows = cols // n_slab
    dma = pltpu.SemaphoreType.DMA
    vmem = pl.BlockSpec(memory_space=pltpu.VMEM)
    hbm = pl.BlockSpec(memory_space=pl.ANY)
    final, updated, basis = pl.pallas_call(
        functools.partial(kernel, n_wide, n_slab, rows_dev * n_wide * n_slab),
        out_shape=(
            jax.ShapeDtypeStruct(state.shape, F32),
            jax.ShapeDtypeStruct(guess.shape, F32),
            jax.ShapeDtypeStruct(panel.shape[1:], F32),
        ),
        in_specs=[hbm, hbm, hbm, vmem, vmem, vmem, vmem],
        out_specs=(hbm, vmem, vmem),
        scratch_shapes=[
            pltpu.VMEM((2, layers, height + 2 * TOP, depth), F32),
            pltpu.VMEM((SWEEPS, 2, height, depth), F32),
            pltpu.VMEM((layers, height, depth), BF16),
            pltpu.VMEM((3, layers, height, depth), BF16),
            pltpu.VMEM((rows_dev, depth), BF16),
            pltpu.VMEM((n_slab, rows_dev, rows_dev), BF16),
            pltpu.VMEM((n_slab, part_rows, cols), F32),
            pltpu.VMEM((n_slab, part_rows, cols), F32),
            pltpu.VMEM((part_rows, cols), F32),
            pltpu.VMEM((n_wide, part_rows, cols), F32),
            pltpu.VMEM((part_rows, cols), F32),
            pltpu.VMEM((n_slab, part_rows, cols), F32),
            pltpu.VMEM((cols, cols), F32),
            pltpu.VMEM((8, rows_dev), F32),
            pltpu.VMEM((n_slab, 8, rows_dev), F32),
            pltpu.VMEM((8, cols), F32),
            pltpu.VMEM((n_slab, 8, cols), F32),
            pltpu.VMEM((8, cols), F32),
            pltpu.VMEM((n_wide, 8, cols), F32),
            dma((4, 3)),
            dma,
            dma((SWEEPS, 2)),
            dma((SWEEPS, 2)),
            dma((3, n_slab)),
            dma((3, n_slab)),
            dma((2, n_wide)),
            dma((2, n_wide)),
            dma((n_slab,)),
            dma((n_slab,)),
        ],
        compiler_params=pltpu.CompilerParams(
            collective_id=0, has_side_effects=True, vmem_limit_bytes=40 * 1024 * 1024
        ),
    )(state, rate, flow, guess, rows, panel[0], output[0])
    return final, updated, basis[None]


def solution(mesh):
    return jax.shard_map(
        functools.partial(shards, mesh.shape["wide"], mesh.shape["slab"]),
        mesh=mesh,
        in_specs=(
            P("wide", "slab", None, None),
            P("wide", "slab", None, None),
            P(None, "wide", "slab", None, None),
            P("wide", "slab"),
            P("wide", "slab"),
            P("wide", "slab", None),
            P("wide", "slab", None),
        ),
        out_specs=(P("wide", "slab", None, None), P("wide", "slab"), P("wide", "slab", None)),
        check_vma=False,
    )
```

```python
import functools
import math

import jax
import jax.numpy as jnp
from jax import lax
from jax.experimental import pallas as pl
from jax.experimental.pallas import tpu as pltpu
from jax.sharding import PartitionSpec as P

INTERFACE_STRIP = 64
SWEEPS = 4
STEP_SIZE = 0.11
TOP = 8
MESH = pl.DeviceIdType.MESH
HIGHEST = lax.Precision.HIGHEST
F32 = jnp.float32
BF16 = jnp.bfloat16


def iota(shape, dim):
    return lax.broadcasted_iota(jnp.int32, shape, dim)


def split3(value):
    hi = value.astype(BF16).astype(F32)
    rest = value - hi
    mid = rest.astype(BF16).astype(F32)
    return hi, mid, rest - mid


def march_rows(source, target, x, y, rate, flow):
    depth = source.shape[2]
    tiles = depth // 128
    rows = pl.ds(TOP + y, 16)
    lane = iota((16, 128), 1)

    def at(c):
        return pl.ds(c * 128, 128)

    zero = jnp.zeros((16, 128), F32)
    centre = source[x, rows, at(0)]
    left_before, left, right = zero, pltpu.roll(centre, 1, 1), pltpu.roll(centre, 127, 1)
    for c in range(tiles):
        if c < tiles - 1:
            after = source[x, rows, at(c + 1)]
            left_after, right_after = pltpu.roll(after, 1, 1), pltpu.roll(after, 127, 1)
        else:
            after = left_after = right_after = zero
        plus_third = jnp.where(lane == 127, right_after, right)
        minus_third = jnp.where(lane == 0, left_before, left)
        plus_first = source[x + 1, rows, at(c)]
        minus_first = source[x - 1, rows, at(c)]
        plus_second = source[x, TOP + y + 1 : TOP + y + 17, at(c)]
        minus_second = source[x, TOP + y - 1 : TOP + y + 15, at(c)]
        spread = (
            (plus_first + minus_first)
            + (plus_second + minus_second)
            + (plus_third + minus_third)
            - 6.0 * centre
        )
        here = (pl.ds(y, 16), at(c))
        carried = (
            flow[(0, x - 1) + here].astype(F32) * (plus_first - minus_first)
            + flow[(1, x - 1) + here].astype(F32) * (plus_second - minus_second)
            + flow[(2, x - 1) + here].astype(F32) * (plus_third - minus_third)
        )
        target[x, rows, at(c)] = centre + STEP_SIZE * (
            rate[(x - 1,) + here].astype(F32) * spread - 0.5 * carried
        )
        left_before, left, right, centre = left, left_after, right_after, after


def eliminate_block(strips, b):
    blocks = len(strips)
    lane = iota((8, 128), 1)
    row = iota((8, 128), 0)
    strips = list(strips)

    def column(s, i):
        return jnp.broadcast_to(s[:, i : i + 1], (8, 128))

    def line(s, i):
        return jnp.broadcast_to(s[i : i + 1, :], (8, 128))

    for i in range(0, 8, 2):
        j = i + 1
        first = [column(s, i) for s in strips]
        second = [column(s, j) for s in strips]
        row_i, row_j = line(strips[0], i), line(strips[0], j)
        over = line(second[0], i)
        inverse_i = 1.0 / line(first[0], i)
        factor = line(first[0], j) * inverse_i
        inverse_j = 1.0 / (line(second[0], j) - factor * over)
        ratio = over * inverse_i
        scaled_i = jnp.where(lane == i, inverse_i, jnp.where(lane == j, 0.0, row_i * inverse_i))
        new_j = jnp.where(lane == i, -factor, row_j - factor * row_i)
        scaled_j = jnp.where(lane == j, inverse_j, new_j * inverse_j)
        pair = (lane == i) | (lane == j)
        updated = [
            jnp.where(pair, 0.0, s) - f * scaled_i - (g - f * ratio) * scaled_j
            for s, f, g in zip(strips, first, second)
        ]
        updated[0] = jnp.where(row > j, updated[0], jnp.where(row == j, new_j, strips[0]))
        strips = updated
    kept = ((lane < 8) & (lane <= row)) | (lane >= 8 * (blocks - b))
    strips[0] = jnp.where(kept, strips[0], 0.0)
    strips = [pltpu.roll(s, 128 - 8, 1) for s in strips]
    return tuple(strips[1:] + strips[:1])


def kernel(
    n_wide,
    n_slab,
    total_rows,
    state_hbm,
    rate_hbm,
    flow_hbm,
    guess_hbm,
    rows_hbm,
    panel_hbm,
    output_hbm,
    final_hbm,
    updated_ref,
    basis_ref,
    guess_ref,
    rows_ref,
    panel_ref,
    output_ref,
    cells_a,
    cells_b,
    rate,
    flow,
    spread_map,
    pick_map,
    gram_own,
    gram_scatter,
    gram_sum,
    gram_wide,
    gram_part,
    gram_full,
    elim,
    face_own,
    face_all,
    proj_own,
    proj_slab,
    proj_sum,
    proj_wide,
    load_sem,
    small_sem,
    store_sem,
    halo_send,
    halo_recv,
    slab_send,
    slab_recv,
    wide_send,
    wide_recv,
    face_send,
    face_recv,
):
    layers, depth = rate.shape[0], rate.shape[2]
    height = rate.shape[1]
    cols = panel_ref.shape[1]
    rows_dev = guess_ref.shape[1]
    per_layer = depth // INTERFACE_STRIP
    part_rows = cols // n_slab
    me_w, me_s = lax.axis_index("wide"), lax.axis_index("slab")
    across = lax.rem(me_w + n_wide // 2, n_wide)

    def slab_peer(k):
        return lax.rem(me_s + k, n_slab)

    def wide_peer(k):
        return lax.rem(me_w + k, n_wide)

    small = [
        pltpu.make_async_copy(source, target, small_sem.at[k])
        for k, (source, target) in enumerate(
            (
                (panel_hbm.at[0], panel_ref),
                (guess_hbm, guess_ref),
                (rows_hbm, rows_ref),
                (output_hbm.at[0], output_ref),
            )
        )
    ]
    for c in small:
        c.start()
    quarter = layers // 4
    loads = {}
    for g in (0, 3, 1, 2):
        planes = pl.ds(g * quarter, quarter)
        loads[g] = [
            pltpu.make_async_copy(
                state_hbm.at[0, planes],
                cells_a.at[pl.ds(1 + g * quarter, quarter), pl.ds(TOP, height)],
                load_sem.at[g, 0],
            ),
            pltpu.make_async_copy(rate_hbm.at[0, planes], rate.at[planes], load_sem.at[g, 1]),
            pltpu.make_async_copy(
                flow_hbm.at[:, 0, planes], flow.at[:, planes], load_sem.at[g, 2]
            ),
        ]
        for c in loads[g]:
            c.start()

    zeros = jnp.zeros((height, depth), F32)
    cells = (cells_a, cells_b)
    for side in range(2):

        @pl.when(me_s == side * (n_slab - 1))
        def _():
            for buffer in cells:
                buffer[side * (layers + 1), TOP : TOP + height, :] = zeros

    barrier = pltpu.get_barrier_semaphore()
    peers = (
        [(me_w, slab_peer(k)) for k in range(1, n_slab)]
        + [(wide_peer(k), me_s) for k in range(1, n_wide)]
        + [(across, slab_peer(k)) for k in range(1, n_slab)]
    )
    for peer in peers:
        pl.semaphore_signal(barrier, inc=1, device_id=peer, device_id_type=MESH)
    pl.semaphore_wait(barrier, len(peers))

    def halo_copies(sweep, low, high):
        down = pltpu.make_async_remote_copy(
            src_ref=low,
            dst_ref=cells[sweep % 2].at[layers + 1, pl.ds(TOP, height)],
            send_sem=halo_send.at[sweep, 0],
            recv_sem=halo_recv.at[sweep, 1],
            device_id=(me_w, lax.max(me_s - 1, 0)),
            device_id_type=MESH,
        )
        up = pltpu.make_async_remote_copy(
            src_ref=high,
            dst_ref=cells[sweep % 2].at[0, pl.ds(TOP, height)],
            send_sem=halo_send.at[sweep, 1],
            recv_sem=halo_recv.at[sweep, 0],
            device_id=(me_w, lax.min(me_s + 1, n_slab - 1)),
            device_id_type=MESH,
        )
        return down, up

    def send_halo(copies):
        @pl.when(me_s > 0)
        def _():
            copies[0].start()

        @pl.when(me_s < n_slab - 1)
        def _():
            copies[1].start()

    def wait_halo(copies):
        @pl.when(me_s > 0)
        def _():
            copies[0].wait_send()
            copies[1].wait_recv()

        @pl.when(me_s < n_slab - 1)
        def _():
            copies[1].wait_send()
            copies[0].wait_recv()

    copies = halo_copies(0, state_hbm.at[0, 0], state_hbm.at[0, layers - 1])
    send_halo(copies)

    def slab_exchange(source, target, phase):
        out = []
        for k in range(1, n_slab):
            c = pltpu.make_async_remote_copy(
                src_ref=source(slab_peer(k)),
                dst_ref=target.at[me_s],
                send_sem=slab_send.at[phase, k],
                recv_sem=slab_recv.at[phase, k],
                device_id=(me_w, slab_peer(k)),
                device_id_type=MESH,
            )
            c.start()
            out.append(c)
        return out

    def wide_exchange(source, target, phase):
        out = []
        for k in range(1, n_wide):
            c = pltpu.make_async_remote_copy(
                src_ref=source,
                dst_ref=target.at[me_w],
                send_sem=wide_send.at[phase, k],
                recv_sem=wide_recv.at[phase, k],
                device_id=(wide_peer(k), me_s),
                device_id_type=MESH,
            )
            c.start()
            out.append(c)
        return out

    def finish(exchange):
        for c in exchange:
            c.wait()

    def summed(ref, count):
        total = ref[0]
        for k in range(1, count):
            total = total + ref[k]
        return total

    small[0].wait()
    panel = panel_ref[...]
    gram = lax.dot_general(
        panel, panel, (((0,), (0,)), ((), ())), precision=HIGHEST, preferred_element_type=F32
    )
    gram_own[...] = gram.reshape(n_slab, part_rows, cols)
    exchange = slab_exchange(lambda peer: gram_own.at[peer], gram_scatter, 0)
    gram_scatter[me_s] = gram_own[me_s]

    line = iota((rows_dev, depth), 0)
    strip = iota((rows_dev, depth), 1) // INTERFACE_STRIP
    spread_map[...] = jnp.where(lax.rem(line, per_layer) == strip, 1.0, 0.0).astype(BF16)
    owner = iota((layers, rows_dev), 1) // per_layer == iota((layers, rows_dev), 0)
    small[1].wait()
    guess = guess_ref[...]
    placed = jnp.where(owner, jnp.broadcast_to(guess, (layers, rows_dev)), 0.0)
    ghost = jnp.zeros((layers, depth), F32)
    for piece in split3(placed):
        ghost = ghost + jnp.dot(piece.astype(BF16), spread_map[...], preferred_element_type=F32)
    empty = jnp.zeros((1, depth), F32)
    for buffer in cells:
        for x in range(layers):
            buffer[1 + x, TOP + height : TOP + height + 1, :] = ghost[x : x + 1, :]
            buffer[1 + x, TOP - 1 : TOP, :] = empty

    def march(sweep, x, ys):
        for y in ys:
            march_rows(cells[sweep % 2], cells[1 - sweep % 2], x, y, rate, flow)

    every = range(0, height, 16)
    blocks = cols // 8
    strips = ()
    for g in (0, 3):
        for c in loads[g]:
            c.wait()
    for sweep in range(SWEEPS - 1):
        wait_halo(copies)
        march(sweep, 1, every)
        march(sweep, layers, every)
        copies = halo_copies(
            sweep + 1,
            cells[1 - sweep % 2].at[1, pl.ds(TOP, height)],
            cells[1 - sweep % 2].at[layers, pl.ds(TOP, height)],
        )
        send_halo(copies)
        if sweep == 0:
            for g in (1, 2):
                for c in loads[g]:
                    c.wait()
        if sweep == SWEEPS - 2:
            finish(exchange)
            square = gram_full[...].reshape(cols, cols)
            strips = tuple(square[8 * t : 8 * t + 8, :] for t in range(blocks))

        def interior(k, strips):
            march(sweep, 2 + 2 * k, every)
            march(sweep, 3 + 2 * k, every)
            return eliminate_block(strips, k) if strips else strips

        strips = lax.fori_loop(0, layers // 2 - 1, interior, strips)
        if sweep == 0:
            finish(exchange)
            gram_sum[...] = summed(gram_scatter, n_slab)
            gram_wide[me_w] = gram_sum[...]
            exchange = wide_exchange(gram_sum, gram_wide, 0)
        elif sweep == 1:
            finish(exchange)
            gram_part[...] = summed(gram_wide, n_wide)
            gram_full[me_s] = gram_part[...]
            exchange = slab_exchange(lambda peer: gram_part, gram_full, 1)
    done = layers // 2 - 1

    wait_halo(copies)

    def upper(k, strips):
        for p in range(4):
            march(SWEEPS - 1, 1 + 4 * k + p, every[1:])
        return eliminate_block(strips, done + k)

    strips = lax.fori_loop(0, layers // 4, upper, strips)
    done += layers // 4

    last = SWEEPS % 2
    face_cells = jnp.concatenate(
        [cells[last][1 + x, TOP + height - 1 : TOP + height, :] for x in range(layers)], axis=0
    )
    sums = jnp.zeros((layers, rows_dev), F32)
    for piece in split3(face_cells):
        sums = sums + lax.dot_general(
            piece.astype(BF16),
            spread_map[...],
            (((1,), (1,)), ((), ())),
            preferred_element_type=F32,
        )
    means = jnp.sum(jnp.where(owner, sums, 0.0), axis=0, keepdims=True) * (1.0 / INTERFACE_STRIP)
    face_own[...] = jnp.broadcast_to(means, (8, rows_dev))
    faces = []
    for k in range(n_slab):
        c = pltpu.make_async_remote_copy(
            src_ref=face_own,
            dst_ref=face_all.at[me_s],
            send_sem=face_send.at[k],
            recv_sem=face_recv.at[k],
            device_id=(across, slab_peer(k)),
            device_id_type=MESH,
        )
        c.start()
        faces.append(c)

    def lower(k, strips):
        for p in range(4):
            march(SWEEPS - 1, 1 + 4 * k + p, every[:1])
        return eliminate_block(strips, done + k)

    strips = lax.fori_loop(0, layers // 4, lower, strips)
    done += layers // 4
    store = pltpu.make_async_copy(
        cells[last].at[pl.ds(1, layers), pl.ds(TOP, height)], final_hbm.at[0], store_sem
    )
    store.start()

    small[2].wait()
    facing = rows_ref[...]
    for s in range(n_slab):
        picked = iota((rows_dev, rows_dev), 0) + s * rows_dev == jnp.broadcast_to(
            facing, (rows_dev, rows_dev)
        )
        pick_map[s] = jnp.where(picked, 1.0, 0.0).astype(BF16)

    finish(faces)
    line8 = iota((8, rows_dev), 0)
    tilde = jnp.zeros((8, rows_dev), F32)
    for s in range(n_slab):
        hi, mid, low = split3(face_all[s])
        triple = jnp.where(line8 == 0, hi, jnp.where(line8 == 1, mid, low))
        triple = jnp.where(line8 < 3, triple, 0.0).astype(BF16)
        tilde = tilde + jnp.dot(triple, pick_map[s], preferred_element_type=F32)
    tilde = jnp.sum(tilde, axis=0, keepdims=True)
    resid = tilde - guess
    proj_own[...] = jnp.dot(
        jnp.broadcast_to(resid, (8, rows_dev)),
        panel_ref[...],
        precision=HIGHEST,
        preferred_element_type=F32,
    )
    proj_slab[me_s] = proj_own[...]
    exchange = slab_exchange(lambda peer: proj_own, proj_slab, 2)
    strips = lax.fori_loop(done, blocks, lambda b, s: eliminate_block(s, b), strips)

    for t in range(blocks):
        on_diagonal = iota((8, cols), 1) == iota((8, cols), 0) + 8 * t
        pivots = jnp.sum(jnp.where(on_diagonal, strips[t], 0.0), axis=1, keepdims=True)
        root = 1.0 / jnp.sqrt(jnp.broadcast_to(pivots, (8, cols)))
        elim[8 * t : 8 * t + 8, :] = jnp.where(on_diagonal, 1.0, strips[t]) * root
    inverse = elim[...]
    finish(exchange)
    proj_sum[...] = summed(proj_slab, n_slab)
    proj_wide[me_w] = proj_sum[...]
    exchange = wide_exchange(proj_sum, proj_wide, 1)
    basis_ref[...] = math.sqrt(total_rows) * lax.dot_general(
        panel_ref[...],
        inverse,
        (((1,), (1,)), ((), ())),
        precision=HIGHEST,
        preferred_element_type=F32,
    )
    small[3].wait()
    turned = lax.dot_general(
        inverse,
        output_ref[...],
        (((1,), (1,)), ((), ())),
        precision=HIGHEST,
        preferred_element_type=F32,
    )
    response = lax.dot_general(
        inverse, turned, (((0,), (0,)), ((), ())), precision=HIGHEST, preferred_element_type=F32
    )
    finish(exchange)
    projection = summed(proj_wide, n_wide)
    update = jnp.dot(projection, response, precision=HIGHEST, preferred_element_type=F32)
    updated_ref[...] = tilde - update[:1, :]
    store.wait()


def shards(n_wide, n_slab, state, rate, flow, guess, rows, panel, output):
    _, layers, height, depth = state.shape
    rows_dev, cols = panel.shape[1:]
    part_rows = cols // n_slab
    dma = pltpu.SemaphoreType.DMA
    vmem = pl.BlockSpec(memory_space=pltpu.VMEM)
    hbm = pl.BlockSpec(memory_space=pltpu.HBM)
    final, updated, basis = pl.pallas_call(
        functools.partial(kernel, n_wide, n_slab, rows_dev * n_wide * n_slab),
        out_shape=(
            jax.ShapeDtypeStruct(state.shape, F32),
            jax.ShapeDtypeStruct(guess.shape, F32),
            jax.ShapeDtypeStruct(panel.shape[1:], F32),
        ),
        in_specs=[hbm] * 7,
        out_specs=(hbm, vmem, vmem),
        scratch_shapes=[
            pltpu.VMEM((1, rows_dev), F32),
            pltpu.VMEM((1, rows_dev), jnp.int32),
            pltpu.VMEM((rows_dev, cols), F32),
            pltpu.VMEM((rows_dev, cols), F32),
            pltpu.VMEM((layers + 2, height + 2 * TOP, depth), F32),
            pltpu.VMEM((layers + 2, height + 2 * TOP, depth), F32),
            pltpu.VMEM((layers, height, depth), BF16),
            pltpu.VMEM((3, layers, height, depth), BF16),
            pltpu.VMEM((rows_dev, depth), BF16),
            pltpu.VMEM((n_slab, rows_dev, rows_dev), BF16),
            pltpu.VMEM((n_slab, part_rows, cols), F32),
            pltpu.VMEM((n_slab, part_rows, cols), F32),
            pltpu.VMEM((part_rows, cols), F32),
            pltpu.VMEM((n_wide, part_rows, cols), F32),
            pltpu.VMEM((part_rows, cols), F32),
            pltpu.VMEM((n_slab, part_rows, cols), F32),
            pltpu.VMEM((cols, cols), F32),
            pltpu.VMEM((8, rows_dev), F32),
            pltpu.VMEM((n_slab, 8, rows_dev), F32),
            pltpu.VMEM((8, cols), F32),
            pltpu.VMEM((n_slab, 8, cols), F32),
            pltpu.VMEM((8, cols), F32),
            pltpu.VMEM((n_wide, 8, cols), F32),
            dma((4, 3)),
            dma((4,)),
            dma,
            dma((SWEEPS, 2)),
            dma((SWEEPS, 2)),
            dma((3, n_slab)),
            dma((3, n_slab)),
            dma((2, n_wide)),
            dma((2, n_wide)),
            dma((n_slab,)),
            dma((n_slab,)),
        ],
        compiler_params=pltpu.CompilerParams(
            collective_id=0, has_side_effects=True, vmem_limit_bytes=56 * 1024 * 1024
        ),
    )(state, rate, flow, guess, rows, panel, output)
    return final, updated, basis[None]


def solution(mesh):
    return jax.shard_map(
        functools.partial(shards, mesh.shape["wide"], mesh.shape["slab"]),
        mesh=mesh,
        in_specs=(
            P("wide", "slab", None, None),
            P("wide", "slab", None, None),
            P(None, "wide", "slab", None, None),
            P("wide", "slab"),
            P("wide", "slab"),
            P("wide", "slab", None),
            P("wide", "slab", None),
        ),
        out_specs=(P("wide", "slab", None, None), P("wide", "slab"), P("wide", "slab", None)),
        check_vma=False,
    )
```

```python
import functools
import math

import jax
import jax.numpy as jnp
from jax import lax
from jax.experimental import pallas as pl
from jax.experimental.pallas import tpu as pltpu
from jax.sharding import PartitionSpec as P

INTERFACE_STRIP = 64
SWEEPS = 4
STEP_SIZE = 0.11
TOP = 8
MESH = pl.DeviceIdType.MESH
HIGHEST = lax.Precision.HIGHEST
F32 = jnp.float32
BF16 = jnp.bfloat16


def iota(shape, dim):
    return lax.broadcasted_iota(jnp.int32, shape, dim)


def split3(value):
    hi = value.astype(BF16).astype(F32)
    rest = value - hi
    mid = rest.astype(BF16).astype(F32)
    return hi, mid, rest - mid


def march_rows(source, store, x, y, factors):
    depth = source.shape[2]
    tiles = depth // 128
    rows = pl.ds(TOP + y, 16)
    lane = iota((16, 128), 1)

    def at(c):
        return pl.ds(c * 128, 128)

    zero = jnp.zeros((16, 128), F32)
    centre = source[x, rows, at(0)]
    left_before, left, right = zero, pltpu.roll(centre, 1, 1), pltpu.roll(centre, 127, 1)
    for c in range(tiles):
        if c < tiles - 1:
            after = source[x, rows, at(c + 1)]
            left_after, right_after = pltpu.roll(after, 1, 1), pltpu.roll(after, 127, 1)
        else:
            after = left_after = right_after = zero
        plus_third = jnp.where(lane == 127, right_after, right)
        minus_third = jnp.where(lane == 0, left_before, left)
        plus_first = source[x + 1, rows, at(c)]
        minus_first = source[x - 1, rows, at(c)]
        plus_second = source[x, TOP + y + 1 : TOP + y + 17, at(c)]
        minus_second = source[x, TOP + y - 1 : TOP + y + 15, at(c)]
        spread = (
            (plus_first + minus_first)
            + (plus_second + minus_second)
            + (plus_third + minus_third)
            - 6.0 * centre
        )
        diffuse, first, second, third = factors(at(c))
        carried = (
            first * (plus_first - minus_first)
            + second * (plus_second - minus_second)
            + third * (plus_third - minus_third)
        )
        store(at(c), centre + (diffuse * spread - carried))
        left_before, left, right, centre = left, left_after, right_after, after


def eliminate_block(strips, b):
    blocks = len(strips)
    lane = iota((8, 128), 1)
    row = iota((8, 128), 0)
    strips = list(strips)

    def column(s, i):
        return jnp.broadcast_to(s[:, i : i + 1], (8, 128))

    def line(s, i):
        return jnp.broadcast_to(s[i : i + 1, :], (8, 128))

    for i in range(0, 8, 2):
        j = i + 1
        first = [column(s, i) for s in strips]
        second = [column(s, j) for s in strips]
        row_i, row_j = line(strips[0], i), line(strips[0], j)
        over = line(second[0], i)
        inverse_i = 1.0 / line(first[0], i)
        factor = line(first[0], j) * inverse_i
        inverse_j = 1.0 / (line(second[0], j) - factor * over)
        ratio = over * inverse_i
        scaled_i = jnp.where(lane == i, inverse_i, jnp.where(lane == j, 0.0, row_i * inverse_i))
        new_j = jnp.where(lane == i, -factor, row_j - factor * row_i)
        scaled_j = jnp.where(lane == j, inverse_j, new_j * inverse_j)
        pair = (lane == i) | (lane == j)
        updated = [
            jnp.where(pair, 0.0, s) - f * scaled_i - (g - f * ratio) * scaled_j
            for s, f, g in zip(strips, first, second)
        ]
        updated[0] = jnp.where(row > j, updated[0], jnp.where(row == j, new_j, strips[0]))
        strips = updated
    kept = ((lane < 8) & (lane <= row)) | (lane >= 8 * (blocks - b))
    strips[0] = jnp.where(kept, strips[0], 0.0)
    strips = [pltpu.roll(s, 128 - 8, 1) for s in strips]
    return tuple(strips[1:] + strips[:1])


def kernel(
    n_wide,
    n_slab,
    total_rows,
    state_hbm,
    rate_hbm,
    flow_hbm,
    guess_hbm,
    rows_hbm,
    panel_hbm,
    output_hbm,
    final_ref,
    updated_ref,
    basis_ref,
    guess_ref,
    rows_ref,
    panel_ref,
    output_ref,
    cells_a,
    cells_b,
    rate,
    flow,
    scaled,
    spread_map,
    pick_map,
    gram_own,
    gram_scatter,
    gram_sum,
    gram_wide,
    gram_part,
    gram_full,
    elim,
    face_own,
    face_all,
    proj_own,
    proj_slab,
    proj_sum,
    proj_wide,
    load_sem,
    small_sem,
    halo_send,
    halo_recv,
    slab_send,
    slab_recv,
    wide_send,
    wide_recv,
    face_send,
    face_recv,
):
    layers, depth = rate.shape[0], rate.shape[2]
    height = rate.shape[1]
    cols = panel_ref.shape[1]
    rows_dev = guess_ref.shape[1]
    per_layer = depth // INTERFACE_STRIP
    part_rows = cols // n_slab
    me_w, me_s = lax.axis_index("wide"), lax.axis_index("slab")
    across = lax.rem(me_w + n_wide // 2, n_wide)

    def slab_peer(k):
        return lax.rem(me_s + k, n_slab)

    def wide_peer(k):
        return lax.rem(me_w + k, n_wide)

    small = [
        pltpu.make_async_copy(source, target, small_sem.at[k])
        for k, (source, target) in enumerate(
            (
                (panel_hbm.at[0], panel_ref),
                (guess_hbm, guess_ref),
                (rows_hbm, rows_ref),
                (output_hbm.at[0], output_ref),
            )
        )
    ]
    for c in small:
        c.start()
    quarter = layers // 4
    loads = {}
    for g in (0, 3, 1, 2):
        planes = pl.ds(g * quarter, quarter)
        loads[g] = [
            pltpu.make_async_copy(
                state_hbm.at[0, planes],
                cells_a.at[pl.ds(1 + g * quarter, quarter), pl.ds(TOP, height)],
                load_sem.at[g, 0],
            ),
            pltpu.make_async_copy(rate_hbm.at[0, planes], rate.at[planes], load_sem.at[g, 1]),
            pltpu.make_async_copy(
                flow_hbm.at[:, 0, planes], flow.at[:, planes], load_sem.at[g, 2]
            ),
        ]
        for c in loads[g]:
            c.start()

    zeros = jnp.zeros((height, depth), F32)
    cells = (cells_a, cells_b)
    for side in range(2):

        @pl.when(me_s == side * (n_slab - 1))
        def _():
            for buffer in cells:
                buffer[side * (layers + 1), TOP : TOP + height, :] = zeros

    barrier = pltpu.get_barrier_semaphore()
    peers = (
        [(me_w, slab_peer(k)) for k in range(1, n_slab)]
        + [(wide_peer(k), me_s) for k in range(1, n_wide)]
        + [(across, slab_peer(k)) for k in range(1, n_slab)]
    )
    for peer in peers:
        pl.semaphore_signal(barrier, inc=1, device_id=peer, device_id_type=MESH)
    pl.semaphore_wait(barrier, len(peers))

    def halo_copies(sweep, low, high):
        down = pltpu.make_async_remote_copy(
            src_ref=low,
            dst_ref=cells[sweep % 2].at[layers + 1, pl.ds(TOP, height)],
            send_sem=halo_send.at[sweep, 0],
            recv_sem=halo_recv.at[sweep, 1],
            device_id=(me_w, lax.max(me_s - 1, 0)),
            device_id_type=MESH,
        )
        up = pltpu.make_async_remote_copy(
            src_ref=high,
            dst_ref=cells[sweep % 2].at[0, pl.ds(TOP, height)],
            send_sem=halo_send.at[sweep, 1],
            recv_sem=halo_recv.at[sweep, 0],
            device_id=(me_w, lax.min(me_s + 1, n_slab - 1)),
            device_id_type=MESH,
        )
        return down, up

    def send_halo(copies):
        @pl.when(me_s > 0)
        def _():
            copies[0].start()

        @pl.when(me_s < n_slab - 1)
        def _():
            copies[1].start()

    def wait_halo(copies):
        @pl.when(me_s > 0)
        def _():
            copies[0].wait_send()
            copies[1].wait_recv()

        @pl.when(me_s < n_slab - 1)
        def _():
            copies[1].wait_send()
            copies[0].wait_recv()

    copies = halo_copies(0, state_hbm.at[0, 0], state_hbm.at[0, layers - 1])
    send_halo(copies)

    def slab_exchange(source, target, phase):
        out = []
        for k in range(1, n_slab):
            c = pltpu.make_async_remote_copy(
                src_ref=source(slab_peer(k)),
                dst_ref=target.at[me_s],
                send_sem=slab_send.at[phase, k],
                recv_sem=slab_recv.at[phase, k],
                device_id=(me_w, slab_peer(k)),
                device_id_type=MESH,
            )
            c.start()
            out.append(c)
        return out

    def wide_exchange(source, target, phase):
        out = []
        for k in range(1, n_wide):
            c = pltpu.make_async_remote_copy(
                src_ref=source,
                dst_ref=target.at[me_w],
                send_sem=wide_send.at[phase, k],
                recv_sem=wide_recv.at[phase, k],
                device_id=(wide_peer(k), me_s),
                device_id_type=MESH,
            )
            c.start()
            out.append(c)
        return out

    def finish(exchange):
        for c in exchange:
            c.wait()

    def summed(ref, count):
        total = ref[0]
        for k in range(1, count):
            total = total + ref[k]
        return total

    small[0].wait()
    panel = panel_ref[...]
    gram = lax.dot_general(
        panel, panel, (((0,), (0,)), ((), ())), precision=HIGHEST, preferred_element_type=F32
    )
    gram_own[...] = gram.reshape(n_slab, part_rows, cols)
    exchange = slab_exchange(lambda peer: gram_own.at[peer], gram_scatter, 0)
    gram_scatter[me_s] = gram_own[me_s]

    line = lax.bitwise_and(iota((rows_dev, 1), 0), per_layer - 1)
    strip = lax.shift_right_logical(iota((1, depth), 1), INTERFACE_STRIP.bit_length() - 1)
    spread_map[...] = jnp.where(line == strip, 1.0, 0.0).astype(BF16)
    owner = lax.shift_right_logical(
        iota((layers, rows_dev), 1), per_layer.bit_length() - 1
    ) == iota((layers, rows_dev), 0)
    small[1].wait()
    guess = guess_ref[...]
    placed = jnp.where(owner, jnp.broadcast_to(guess, (layers, rows_dev)), 0.0)
    pieces = jnp.dot(
        jnp.concatenate(split3(placed), axis=0).astype(BF16),
        spread_map[...],
        preferred_element_type=F32,
    )
    ghost = pieces[:layers] + pieces[layers : 2 * layers] + pieces[2 * layers :]
    empty = jnp.zeros((1, depth), F32)
    for buffer in cells:
        for x in range(layers):
            buffer[1 + x, TOP + height : TOP + height + 1, :] = ghost[x : x + 1, :]
            buffer[1 + x, TOP - 1 : TOP, :] = empty

    def march(sweep, x, ys):
        source, target = cells[sweep % 2], cells[1 - sweep % 2]
        for y in ys:
            rows = pl.ds(y, 16)

            def factors(lanes):
                if sweep:
                    return [scaled[d, x - 1, rows, lanes] for d in range(4)]
                found = [STEP_SIZE * rate[x - 1, rows, lanes].astype(F32)] + [
                    (0.5 * STEP_SIZE) * flow[d, x - 1, rows, lanes].astype(F32) for d in range(3)
                ]
                for d in range(4):
                    scaled[d, x - 1, rows, lanes] = found[d]
                return found

            def store(lanes, value):
                if sweep == SWEEPS - 1:
                    final_ref[0, x - 1, rows, lanes] = value
                else:
                    target[x, pl.ds(TOP + y, 16), lanes] = value

            march_rows(source, store, x, y, factors)

    every = range(0, height, 16)
    blocks = cols // 8
    strips = ()
    for g in (0, 3):
        for c in loads[g]:
            c.wait()
    for sweep in range(SWEEPS - 1):
        wait_halo(copies)
        march(sweep, 1, every)
        march(sweep, layers, every)
        copies = halo_copies(
            sweep + 1,
            cells[1 - sweep % 2].at[1, pl.ds(TOP, height)],
            cells[1 - sweep % 2].at[layers, pl.ds(TOP, height)],
        )
        send_halo(copies)
        if sweep == 0:
            for g in (1, 2):
                for c in loads[g]:
                    c.wait()
        finish(exchange)
        if sweep == 0:
            gram_sum[...] = summed(gram_scatter, n_slab)
            gram_wide[me_w] = gram_sum[...]
            exchange = wide_exchange(gram_sum, gram_wide, 0)
        elif sweep == 1:
            gram_part[...] = summed(gram_wide, n_wide)
            gram_full[me_s] = gram_part[...]
            exchange = slab_exchange(lambda peer: gram_part, gram_full, 1)
        else:
            square = gram_full[...].reshape(cols, cols)
            strips = tuple(square[8 * t : 8 * t + 8, :] for t in range(blocks))

        def interior(k, strips):
            march(sweep, 2 + 2 * k, every)
            march(sweep, 3 + 2 * k, every)
            return eliminate_block(strips, k) if strips else strips

        strips = lax.fori_loop(0, layers // 2 - 1, interior, strips)
    done = layers // 2 - 1

    wait_halo(copies)

    def upper(k, _):
        march(SWEEPS - 1, 1 + 2 * k, every[1:])
        march(SWEEPS - 1, 2 + 2 * k, every[1:])
        return 0

    lax.fori_loop(0, layers // 2, upper, 0)

    face_cells = jnp.concatenate(
        [final_ref[0, x, height - 1 : height, :] for x in range(layers)], axis=0
    )
    sums = lax.dot_general(
        jnp.concatenate(split3(face_cells), axis=0).astype(BF16),
        spread_map[...],
        (((1,), (1,)), ((), ())),
        preferred_element_type=F32,
    )
    sums = sums[:layers] + sums[layers : 2 * layers] + sums[2 * layers :]
    means = jnp.sum(jnp.where(owner, sums, 0.0), axis=0, keepdims=True) * (1.0 / INTERFACE_STRIP)
    face_own[...] = jnp.broadcast_to(means, (8, rows_dev))
    faces = []
    for k in range(n_slab):
        c = pltpu.make_async_remote_copy(
            src_ref=face_own,
            dst_ref=face_all.at[me_s],
            send_sem=face_send.at[k],
            recv_sem=face_recv.at[k],
            device_id=(across, slab_peer(k)),
            device_id_type=MESH,
        )
        c.start()
        faces.append(c)

    small[2].wait()
    facing = rows_ref[...]
    for s in range(n_slab):
        picked = iota((rows_dev, rows_dev), 0) + s * rows_dev == jnp.broadcast_to(
            facing, (rows_dev, rows_dev)
        )
        pick_map[s] = jnp.where(picked, 1.0, 0.0).astype(BF16)

    def lower(k, strips):
        march(SWEEPS - 1, 1 + 2 * k, every[:1])
        march(SWEEPS - 1, 2 + 2 * k, every[:1])
        return eliminate_block(strips, done + k)

    pairs = layers // 2
    strips = lax.fori_loop(0, pairs // 3 + 1, lower, strips)

    finish(faces)
    line8 = iota((8, rows_dev), 0)
    tilde = jnp.zeros((8, rows_dev), F32)
    for s in range(n_slab):
        hi, mid, low = split3(face_all[s])
        triple = jnp.where(line8 == 0, hi, jnp.where(line8 == 1, mid, low))
        triple = jnp.where(line8 < 3, triple, 0.0).astype(BF16)
        tilde = tilde + jnp.dot(triple, pick_map[s], preferred_element_type=F32)
    tilde = jnp.sum(tilde, axis=0, keepdims=True)
    resid = tilde - guess
    proj_own[...] = jnp.dot(
        jnp.broadcast_to(resid, (8, rows_dev)),
        panel_ref[...],
        precision=HIGHEST,
        preferred_element_type=F32,
    )
    proj_slab[me_s] = proj_own[...]
    exchange = slab_exchange(lambda peer: proj_own, proj_slab, 2)
    strips = lax.fori_loop(pairs // 3 + 1, 2 * (pairs // 3 + 1), lower, strips)
    finish(exchange)
    proj_sum[...] = summed(proj_slab, n_slab)
    proj_wide[me_w] = proj_sum[...]
    exchange = wide_exchange(proj_sum, proj_wide, 1)
    strips = lax.fori_loop(2 * (pairs // 3 + 1), pairs, lower, strips)
    strips = lax.fori_loop(done + pairs, blocks, lambda b, s: eliminate_block(s, b), strips)

    for t in range(blocks):
        on_diagonal = iota((8, cols), 1) == iota((8, cols), 0) + 8 * t
        pivots = jnp.sum(jnp.where(on_diagonal, strips[t], 0.0), axis=1, keepdims=True)
        root = 1.0 / jnp.sqrt(jnp.broadcast_to(pivots, (8, cols)))
        elim[8 * t : 8 * t + 8, :] = jnp.where(on_diagonal, 1.0, strips[t]) * root
    inverse = elim[...]
    basis_ref[...] = math.sqrt(total_rows) * lax.dot_general(
        panel_ref[...],
        inverse,
        (((1,), (1,)), ((), ())),
        precision=HIGHEST,
        preferred_element_type=F32,
    )
    small[3].wait()
    turned = lax.dot_general(
        inverse,
        output_ref[...],
        (((1,), (1,)), ((), ())),
        precision=HIGHEST,
        preferred_element_type=F32,
    )
    response = lax.dot_general(
        inverse, turned, (((0,), (0,)), ((), ())), precision=HIGHEST, preferred_element_type=F32
    )
    finish(exchange)
    projection = summed(proj_wide, n_wide)
    update = jnp.dot(projection, response, precision=HIGHEST, preferred_element_type=F32)
    updated_ref[...] = tilde - update[:1, :]


def put(final_ref, updated_ref, basis_ref, final_hbm, updated_hbm, basis_hbm, sem):
    copies = [
        pltpu.make_async_copy(source, target, sem.at[k])
        for k, (source, target) in enumerate(
            ((final_ref, final_hbm), (updated_ref, updated_hbm), (basis_ref, basis_hbm))
        )
    ]
    for c in copies:
        c.start()
    for c in copies:
        c.wait()


def shards(n_wide, n_slab, state, rate, flow, guess, rows, panel, output):
    _, layers, height, depth = state.shape
    rows_dev, cols = panel.shape[1:]
    part_rows = cols // n_slab
    dma = pltpu.SemaphoreType.DMA
    vmem = pl.BlockSpec(memory_space=pltpu.VMEM)
    hbm = pl.BlockSpec(memory_space=pltpu.HBM)
    final, updated, basis = pl.pallas_call(
        functools.partial(kernel, n_wide, n_slab, rows_dev * n_wide * n_slab),
        out_shape=(
            jax.ShapeDtypeStruct(state.shape, F32),
            jax.ShapeDtypeStruct(guess.shape, F32),
            jax.ShapeDtypeStruct(panel.shape[1:], F32),
        ),
        in_specs=[hbm] * 7,
        out_specs=(vmem, vmem, vmem),
        scratch_shapes=[
            pltpu.VMEM((1, rows_dev), F32),
            pltpu.VMEM((1, rows_dev), jnp.int32),
            pltpu.VMEM((rows_dev, cols), F32),
            pltpu.VMEM((rows_dev, cols), F32),
            pltpu.VMEM((layers + 2, height + 2 * TOP, depth), F32),
            pltpu.VMEM((layers + 2, height + 2 * TOP, depth), F32),
            pltpu.VMEM((layers, height, depth), BF16),
            pltpu.VMEM((3, layers, height, depth), BF16),
            pltpu.VMEM((4, layers, height, depth), F32),
            pltpu.VMEM((rows_dev, depth), BF16),
            pltpu.VMEM((n_slab, rows_dev, rows_dev), BF16),
            pltpu.VMEM((n_slab, part_rows, cols), F32),
            pltpu.VMEM((n_slab, part_rows, cols), F32),
            pltpu.VMEM((part_rows, cols), F32),
            pltpu.VMEM((n_wide, part_rows, cols), F32),
            pltpu.VMEM((part_rows, cols), F32),
            pltpu.VMEM((n_slab, part_rows, cols), F32),
            pltpu.VMEM((cols, cols), F32),
            pltpu.VMEM((8, rows_dev), F32),
            pltpu.VMEM((n_slab, 8, rows_dev), F32),
            pltpu.VMEM((8, cols), F32),
            pltpu.VMEM((n_slab, 8, cols), F32),
            pltpu.VMEM((8, cols), F32),
            pltpu.VMEM((n_wide, 8, cols), F32),
            dma((4, 3)),
            dma((4,)),
            dma((SWEEPS, 2)),
            dma((SWEEPS, 2)),
            dma((3, n_slab)),
            dma((3, n_slab)),
            dma((2, n_wide)),
            dma((2, n_wide)),
            dma((n_slab,)),
            dma((n_slab,)),
        ],
        compiler_params=pltpu.CompilerParams(
            collective_id=0, has_side_effects=True, vmem_limit_bytes=44 * 1024 * 1024
        ),
    )(
        *(
            pltpu.with_memory_space_constraint(value, pltpu.HBM)
            for value in (state, rate, flow, guess, rows, panel, output)
        )
    )
    outs = (final, updated, basis[None])
    return pl.pallas_call(
        put,
        out_shape=tuple(jax.ShapeDtypeStruct(o.shape, F32) for o in outs),
        in_specs=[vmem] * 3,
        out_specs=(hbm,) * 3,
        scratch_shapes=[dma((3,))],
        compiler_params=pltpu.CompilerParams(vmem_limit_bytes=16 * 1024 * 1024),
    )(*outs)


def solution(mesh):
    return jax.shard_map(
        functools.partial(shards, mesh.shape["wide"], mesh.shape["slab"]),
        mesh=mesh,
        in_specs=(
            P("wide", "slab", None, None),
            P("wide", "slab", None, None),
            P(None, "wide", "slab", None, None),
            P("wide", "slab"),
            P("wide", "slab"),
            P("wide", "slab", None),
            P("wide", "slab", None),
        ),
        out_specs=(P("wide", "slab", None, None), P("wide", "slab"), P("wide", "slab", None)),
        check_vma=False,
    )
```

```python
import functools
import math

import jax
import jax.numpy as jnp
from jax import lax
from jax.experimental import pallas as pl
from jax.experimental.pallas import tpu as pltpu
from jax.sharding import PartitionSpec as P

INTERFACE_STRIP = 64
SWEEPS = 4
STEP_SIZE = 0.11
TOP = 8
MESH = pl.DeviceIdType.MESH
HIGHEST = lax.Precision.HIGHEST
F32 = jnp.float32
BF16 = jnp.bfloat16


def iota(shape, dim):
    return lax.broadcasted_iota(jnp.int32, shape, dim)


def split3(value):
    hi = value.astype(BF16).astype(F32)
    rest = value - hi
    mid = rest.astype(BF16).astype(F32)
    return hi, mid, rest - mid


def march_rows(source, store, x, y, factors):
    depth = source.shape[2]
    tiles = depth // 128
    rows = pl.ds(TOP + y, 16)
    lane = iota((16, 128), 1)

    def at(c):
        return pl.ds(c * 128, 128)

    zero = jnp.zeros((16, 128), F32)
    centre = source[x, rows, at(0)]
    left_before, left, right = zero, pltpu.roll(centre, 1, 1), pltpu.roll(centre, 127, 1)
    for c in range(tiles):
        if c < tiles - 1:
            after = source[x, rows, at(c + 1)]
            left_after, right_after = pltpu.roll(after, 1, 1), pltpu.roll(after, 127, 1)
        else:
            after = left_after = right_after = zero
        plus_third = jnp.where(lane == 127, right_after, right)
        minus_third = jnp.where(lane == 0, left_before, left)
        plus_first = source[x + 1, rows, at(c)]
        minus_first = source[x - 1, rows, at(c)]
        plus_second = source[x, TOP + y + 1 : TOP + y + 17, at(c)]
        minus_second = source[x, TOP + y - 1 : TOP + y + 15, at(c)]
        spread = (
            (plus_first + minus_first)
            + (plus_second + minus_second)
            + (plus_third + minus_third)
            - 6.0 * centre
        )
        diffuse, first, second, third = factors(at(c))
        carried = (
            first * (plus_first - minus_first)
            + second * (plus_second - minus_second)
            + third * (plus_third - minus_third)
        )
        store(at(c), centre + (diffuse * spread - carried))
        left_before, left, right, centre = left, left_after, right_after, after


def reciprocal(value):
    near = pl.reciprocal(value, approx=True)
    for _ in range(2):
        near = near + near * (1.0 - value * near)
    return near


def eliminate_block(strips, b, active):
    blocks = len(strips)
    lane = iota((8, 128), 1)
    row = iota((8, 128), 0)
    strips, finished = list(strips[:active]), list(strips[active:])

    def column(s, i):
        return jnp.broadcast_to(s[:, i : i + 1], (8, 128))

    def line(s, i):
        return jnp.broadcast_to(s[i : i + 1, :], (8, 128))

    for i in range(0, 8, 2):
        j = i + 1
        first = [column(s, i) for s in strips]
        second = [column(s, j) for s in strips]
        row_i, row_j = line(strips[0], i), line(strips[0], j)
        over = line(second[0], i)
        inverse_i = reciprocal(line(first[0], i))
        factor = line(first[0], j) * inverse_i
        inverse_j = reciprocal(line(second[0], j) - factor * over)
        ratio = over * inverse_i
        scaled_i = jnp.where(lane == i, inverse_i, jnp.where(lane == j, 0.0, row_i * inverse_i))
        new_j = jnp.where(lane == i, -factor, row_j - factor * row_i)
        scaled_j = jnp.where(lane == j, inverse_j, new_j * inverse_j)
        pair = (lane == i) | (lane == j)
        updated = [
            jnp.where(pair, 0.0, s) - f * scaled_i - (g - f * ratio) * scaled_j
            for s, f, g in zip(strips, first, second)
        ]
        updated[0] = jnp.where(row > j, updated[0], jnp.where(row == j, new_j, strips[0]))
        strips = updated
    kept = ((lane < 8) & (lane <= row)) | (lane >= 8 * (blocks - b))
    strips[0] = jnp.where(kept, strips[0], 0.0)
    strips = [pltpu.roll(s, 128 - 8, 1) for s in strips + finished]
    return tuple(strips[1:] + strips[:1])


def kernel(
    n_wide,
    n_slab,
    total_rows,
    state_hbm,
    rate_hbm,
    flow_hbm,
    guess_hbm,
    rows_hbm,
    panel_hbm,
    output_hbm,
    final_ref,
    updated_ref,
    basis_ref,
    guess_ref,
    rows_ref,
    panel_ref,
    output_ref,
    cells_a,
    cells_b,
    rate,
    flow,
    scaled,
    spread_map,
    pick_map,
    gram_own,
    gram_scatter,
    gram_sum,
    gram_wide,
    gram_part,
    gram_full,
    elim,
    face_own,
    face_all,
    proj_own,
    proj_slab,
    proj_sum,
    proj_wide,
    load_sem,
    small_sem,
    halo_send,
    halo_recv,
    slab_send,
    slab_recv,
    wide_send,
    wide_recv,
    face_send,
    face_recv,
):
    layers, depth = rate.shape[0], rate.shape[2]
    height = rate.shape[1]
    cols = panel_ref.shape[1]
    rows_dev = guess_ref.shape[1]
    per_layer = depth // INTERFACE_STRIP
    part_rows = cols // n_slab
    me_w, me_s = lax.axis_index("wide"), lax.axis_index("slab")
    across = lax.rem(me_w + n_wide // 2, n_wide)

    def slab_peer(k):
        return lax.rem(me_s + k, n_slab)

    def wide_peer(k):
        return lax.rem(me_w + k, n_wide)

    small = [
        pltpu.make_async_copy(source, target, small_sem.at[k])
        for k, (source, target) in enumerate(
            (
                (panel_hbm.at[0], panel_ref),
                (guess_hbm, guess_ref),
                (rows_hbm, rows_ref),
                (output_hbm.at[0], output_ref),
            )
        )
    ]
    for c in small:
        c.start()
    quarter = layers // 4
    loads = {}
    for g in (0, 3, 1, 2):
        planes = pl.ds(g * quarter, quarter)
        loads[g] = [
            pltpu.make_async_copy(
                state_hbm.at[0, planes],
                cells_a.at[pl.ds(1 + g * quarter, quarter), pl.ds(TOP, height)],
                load_sem.at[g, 0],
            ),
            pltpu.make_async_copy(rate_hbm.at[0, planes], rate.at[planes], load_sem.at[g, 1]),
            pltpu.make_async_copy(
                flow_hbm.at[:, 0, planes], flow.at[:, planes], load_sem.at[g, 2]
            ),
        ]
        for c in loads[g]:
            c.start()

    zeros = jnp.zeros((height, depth), F32)
    cells = (cells_a, cells_b)
    for side in range(2):

        @pl.when(me_s == side * (n_slab - 1))
        def _():
            for buffer in cells:
                buffer[side * (layers + 1), TOP : TOP + height, :] = zeros

    barrier = pltpu.get_barrier_semaphore()
    peers = (
        [(me_w, slab_peer(k)) for k in range(1, n_slab)]
        + [(wide_peer(k), me_s) for k in range(1, n_wide)]
        + [(across, slab_peer(k)) for k in range(1, n_slab)]
    )
    for peer in peers:
        pl.semaphore_signal(barrier, inc=1, device_id=peer, device_id_type=MESH)
    pl.semaphore_wait(barrier, len(peers))

    def halo_copies(sweep, low, high):
        down = pltpu.make_async_remote_copy(
            src_ref=low,
            dst_ref=cells[sweep % 2].at[layers + 1, pl.ds(TOP, height)],
            send_sem=halo_send.at[sweep, 0],
            recv_sem=halo_recv.at[sweep, 1],
            device_id=(me_w, lax.max(me_s - 1, 0)),
            device_id_type=MESH,
        )
        up = pltpu.make_async_remote_copy(
            src_ref=high,
            dst_ref=cells[sweep % 2].at[0, pl.ds(TOP, height)],
            send_sem=halo_send.at[sweep, 1],
            recv_sem=halo_recv.at[sweep, 0],
            device_id=(me_w, lax.min(me_s + 1, n_slab - 1)),
            device_id_type=MESH,
        )
        return down, up

    def send_halo(copies):
        @pl.when(me_s > 0)
        def _():
            copies[0].start()

        @pl.when(me_s < n_slab - 1)
        def _():
            copies[1].start()

    def wait_halo(copies):
        @pl.when(me_s > 0)
        def _():
            copies[0].wait_send()
            copies[1].wait_recv()

        @pl.when(me_s < n_slab - 1)
        def _():
            copies[1].wait_send()
            copies[0].wait_recv()

    copies = halo_copies(0, state_hbm.at[0, 0], state_hbm.at[0, layers - 1])
    send_halo(copies)

    def slab_exchange(source, target, phase):
        out = []
        for k in range(1, n_slab):
            c = pltpu.make_async_remote_copy(
                src_ref=source(slab_peer(k)),
                dst_ref=target.at[me_s],
                send_sem=slab_send.at[phase, k],
                recv_sem=slab_recv.at[phase, k],
                device_id=(me_w, slab_peer(k)),
                device_id_type=MESH,
            )
            c.start()
            out.append(c)
        return out

    def wide_exchange(source, target, phase):
        out = []
        for k in range(1, n_wide):
            c = pltpu.make_async_remote_copy(
                src_ref=source,
                dst_ref=target.at[me_w],
                send_sem=wide_send.at[phase, k],
                recv_sem=wide_recv.at[phase, k],
                device_id=(wide_peer(k), me_s),
                device_id_type=MESH,
            )
            c.start()
            out.append(c)
        return out

    def finish(exchange):
        for c in exchange:
            c.wait()

    def summed(ref, count):
        total = ref[0]
        for k in range(1, count):
            total = total + ref[k]
        return total

    small[0].wait()
    panel = panel_ref[...]
    gram = lax.dot_general(
        panel, panel, (((0,), (0,)), ((), ())), precision=HIGHEST, preferred_element_type=F32
    )
    gram_own[...] = gram.reshape(n_slab, part_rows, cols)
    exchange = slab_exchange(lambda peer: gram_own.at[peer], gram_scatter, 0)
    gram_scatter[me_s] = gram_own[me_s]

    line = lax.bitwise_and(iota((rows_dev, 1), 0), per_layer - 1)
    strip = lax.shift_right_logical(iota((1, depth), 1), INTERFACE_STRIP.bit_length() - 1)
    spread_map[...] = jnp.where(line == strip, 1.0, 0.0).astype(BF16)
    owner = lax.shift_right_logical(
        iota((layers, rows_dev), 1), per_layer.bit_length() - 1
    ) == iota((layers, rows_dev), 0)
    small[1].wait()
    guess = guess_ref[...]
    placed = jnp.where(owner, jnp.broadcast_to(guess, (layers, rows_dev)), 0.0)
    pieces = jnp.dot(
        jnp.concatenate(split3(placed), axis=0).astype(BF16),
        spread_map[...],
        preferred_element_type=F32,
    )
    ghost = pieces[:layers] + pieces[layers : 2 * layers] + pieces[2 * layers :]
    empty = jnp.zeros((1, depth), F32)
    for buffer in cells:
        for x in range(layers):
            buffer[1 + x, TOP + height : TOP + height + 1, :] = ghost[x : x + 1, :]
            buffer[1 + x, TOP - 1 : TOP, :] = empty

    def march(sweep, x, ys):
        source, target = cells[sweep % 2], cells[1 - sweep % 2]
        for y in ys:
            rows = pl.ds(y, 16)

            def factors(lanes):
                if sweep:
                    return [scaled[d, x - 1, rows, lanes] for d in range(4)]
                found = [STEP_SIZE * rate[x - 1, rows, lanes].astype(F32)] + [
                    (0.5 * STEP_SIZE) * flow[d, x - 1, rows, lanes].astype(F32) for d in range(3)
                ]
                for d in range(4):
                    scaled[d, x - 1, rows, lanes] = found[d]
                return found

            def store(lanes, value):
                if sweep == SWEEPS - 1:
                    final_ref[0, x - 1, rows, lanes] = value
                else:
                    target[x, pl.ds(TOP + y, 16), lanes] = value

            march_rows(source, store, x, y, factors)

    every = range(0, height, 16)
    blocks = cols // 8
    strips = ()
    for g in (0, 3):
        for c in loads[g]:
            c.wait()
    for sweep in range(SWEEPS - 1):
        wait_halo(copies)
        march(sweep, 1, every)
        march(sweep, layers, every)
        copies = halo_copies(
            sweep + 1,
            cells[1 - sweep % 2].at[1, pl.ds(TOP, height)],
            cells[1 - sweep % 2].at[layers, pl.ds(TOP, height)],
        )
        send_halo(copies)
        if sweep == 0:
            for g in (1, 2):
                for c in loads[g]:
                    c.wait()
        finish(exchange)
        if sweep == 0:
            gram_sum[...] = summed(gram_scatter, n_slab)
            gram_wide[me_w] = gram_sum[...]
            exchange = wide_exchange(gram_sum, gram_wide, 0)
        elif sweep == 1:
            gram_part[...] = summed(gram_wide, n_wide)
            gram_full[me_s] = gram_part[...]
            exchange = slab_exchange(lambda peer: gram_part, gram_full, 1)
        else:
            square = gram_full[...].reshape(cols, cols)
            strips = tuple(square[8 * t : 8 * t + 8, :] for t in range(blocks))

        def interior(first, k, strips):
            march(sweep, 2 + 2 * k, every)
            march(sweep, 3 + 2 * k, every)
            return eliminate_block(strips, k, blocks - first) if strips else strips

        cuts = (0, layers // 4, layers // 2 - 1) if strips else (0, layers // 2 - 1)
        for first, end in zip(cuts, cuts[1:]):
            strips = lax.fori_loop(first, end, functools.partial(interior, first), strips)
    done = layers // 2 - 1

    wait_halo(copies)

    def upper(k, _):
        march(SWEEPS - 1, 1 + 2 * k, every[1:])
        march(SWEEPS - 1, 2 + 2 * k, every[1:])
        return 0

    lax.fori_loop(0, layers // 2, upper, 0)

    face_cells = jnp.concatenate(
        [final_ref[0, x, height - 1 : height, :] for x in range(layers)], axis=0
    )
    sums = lax.dot_general(
        jnp.concatenate(split3(face_cells), axis=0).astype(BF16),
        spread_map[...],
        (((1,), (1,)), ((), ())),
        preferred_element_type=F32,
    )
    sums = sums[:layers] + sums[layers : 2 * layers] + sums[2 * layers :]
    means = jnp.sum(jnp.where(owner, sums, 0.0), axis=0, keepdims=True) * (1.0 / INTERFACE_STRIP)
    face_own[...] = jnp.broadcast_to(means, (8, rows_dev))
    faces = []
    for k in range(n_slab):
        c = pltpu.make_async_remote_copy(
            src_ref=face_own,
            dst_ref=face_all.at[me_s],
            send_sem=face_send.at[k],
            recv_sem=face_recv.at[k],
            device_id=(across, slab_peer(k)),
            device_id_type=MESH,
        )
        c.start()
        faces.append(c)

    small[2].wait()
    facing = rows_ref[...]
    for s in range(n_slab):
        picked = iota((rows_dev, rows_dev), 0) + s * rows_dev == jnp.broadcast_to(
            facing, (rows_dev, rows_dev)
        )
        pick_map[s] = jnp.where(picked, 1.0, 0.0).astype(BF16)

    def lower(first, k, strips):
        march(SWEEPS - 1, 1 + 2 * k, every[:1])
        march(SWEEPS - 1, 2 + 2 * k, every[:1])
        return eliminate_block(strips, done + k, blocks - done - first)

    pairs = layers // 2
    part = pairs // 3 + 1
    strips = lax.fori_loop(0, part, functools.partial(lower, 0), strips)

    finish(faces)
    line8 = iota((8, rows_dev), 0)
    tilde = jnp.zeros((8, rows_dev), F32)
    for s in range(n_slab):
        hi, mid, low = split3(face_all[s])
        triple = jnp.where(line8 == 0, hi, jnp.where(line8 == 1, mid, low))
        triple = jnp.where(line8 < 3, triple, 0.0).astype(BF16)
        tilde = tilde + jnp.dot(triple, pick_map[s], preferred_element_type=F32)
    tilde = jnp.sum(tilde, axis=0, keepdims=True)
    resid = tilde - guess
    proj_own[...] = jnp.dot(
        jnp.broadcast_to(resid, (8, rows_dev)),
        panel_ref[...],
        precision=HIGHEST,
        preferred_element_type=F32,
    )
    proj_slab[me_s] = proj_own[...]
    exchange = slab_exchange(lambda peer: proj_own, proj_slab, 2)
    strips = lax.fori_loop(part, 2 * part, functools.partial(lower, part), strips)
    finish(exchange)
    proj_sum[...] = summed(proj_slab, n_slab)
    proj_wide[me_w] = proj_sum[...]
    exchange = wide_exchange(proj_sum, proj_wide, 1)
    strips = lax.fori_loop(2 * part, pairs, functools.partial(lower, 2 * part), strips)
    for b in range(done + pairs, blocks):
        strips = eliminate_block(strips, b, blocks - b)

    for t in range(blocks):
        on_diagonal = iota((8, cols), 1) == iota((8, cols), 0) + 8 * t
        pivots = jnp.sum(jnp.where(on_diagonal, strips[t], 0.0), axis=1, keepdims=True)
        root = 1.0 / jnp.sqrt(jnp.broadcast_to(pivots, (8, cols)))
        elim[8 * t : 8 * t + 8, :] = jnp.where(on_diagonal, 1.0, strips[t]) * root
    inverse = elim[...]
    basis_ref[...] = math.sqrt(total_rows) * lax.dot_general(
        panel_ref[...],
        inverse,
        (((1,), (1,)), ((), ())),
        precision=HIGHEST,
        preferred_element_type=F32,
    )
    small[3].wait()
    turned = lax.dot_general(
        inverse,
        output_ref[...],
        (((1,), (1,)), ((), ())),
        precision=HIGHEST,
        preferred_element_type=F32,
    )
    response = lax.dot_general(
        inverse, turned, (((0,), (0,)), ((), ())), precision=HIGHEST, preferred_element_type=F32
    )
    finish(exchange)
    projection = summed(proj_wide, n_wide)
    update = jnp.dot(projection, response, precision=HIGHEST, preferred_element_type=F32)
    updated_ref[...] = tilde - update[:1, :]


def put(final_ref, updated_ref, basis_ref, final_hbm, updated_hbm, basis_hbm, sem):
    copies = [
        pltpu.make_async_copy(source, target, sem.at[k])
        for k, (source, target) in enumerate(
            ((final_ref, final_hbm), (updated_ref, updated_hbm), (basis_ref, basis_hbm))
        )
    ]
    for c in copies:
        c.start()
    for c in copies:
        c.wait()


def shards(n_wide, n_slab, state, rate, flow, guess, rows, panel, output):
    _, layers, height, depth = state.shape
    rows_dev, cols = panel.shape[1:]
    part_rows = cols // n_slab
    dma = pltpu.SemaphoreType.DMA
    vmem = pl.BlockSpec(memory_space=pltpu.VMEM)
    hbm = pl.BlockSpec(memory_space=pltpu.HBM)
    final, updated, basis = pl.pallas_call(
        functools.partial(kernel, n_wide, n_slab, rows_dev * n_wide * n_slab),
        out_shape=(
            jax.ShapeDtypeStruct(state.shape, F32),
            jax.ShapeDtypeStruct(guess.shape, F32),
            jax.ShapeDtypeStruct(panel.shape[1:], F32),
        ),
        in_specs=[hbm] * 7,
        out_specs=(vmem, vmem, vmem),
        scratch_shapes=[
            pltpu.VMEM((1, rows_dev), F32),
            pltpu.VMEM((1, rows_dev), jnp.int32),
            pltpu.VMEM((rows_dev, cols), F32),
            pltpu.VMEM((rows_dev, cols), F32),
            pltpu.VMEM((layers + 2, height + 2 * TOP, depth), F32),
            pltpu.VMEM((layers + 2, height + 2 * TOP, depth), F32),
            pltpu.VMEM((layers, height, depth), BF16),
            pltpu.VMEM((3, layers, height, depth), BF16),
            pltpu.VMEM((4, layers, height, depth), F32),
            pltpu.VMEM((rows_dev, depth), BF16),
            pltpu.VMEM((n_slab, rows_dev, rows_dev), BF16),
            pltpu.VMEM((n_slab, part_rows, cols), F32),
            pltpu.VMEM((n_slab, part_rows, cols), F32),
            pltpu.VMEM((part_rows, cols), F32),
            pltpu.VMEM((n_wide, part_rows, cols), F32),
            pltpu.VMEM((part_rows, cols), F32),
            pltpu.VMEM((n_slab, part_rows, cols), F32),
            pltpu.VMEM((cols, cols), F32),
            pltpu.VMEM((8, rows_dev), F32),
            pltpu.VMEM((n_slab, 8, rows_dev), F32),
            pltpu.VMEM((8, cols), F32),
            pltpu.VMEM((n_slab, 8, cols), F32),
            pltpu.VMEM((8, cols), F32),
            pltpu.VMEM((n_wide, 8, cols), F32),
            dma((4, 3)),
            dma((4,)),
            dma((SWEEPS, 2)),
            dma((SWEEPS, 2)),
            dma((3, n_slab)),
            dma((3, n_slab)),
            dma((2, n_wide)),
            dma((2, n_wide)),
            dma((n_slab,)),
            dma((n_slab,)),
        ],
        compiler_params=pltpu.CompilerParams(
            collective_id=0, has_side_effects=True, vmem_limit_bytes=44 * 1024 * 1024
        ),
    )(
        *(
            pltpu.with_memory_space_constraint(value, pltpu.HBM)
            for value in (state, rate, flow, guess, rows, panel, output)
        )
    )
    outs = (final, updated, basis[None])
    return pl.pallas_call(
        put,
        out_shape=tuple(jax.ShapeDtypeStruct(o.shape, F32) for o in outs),
        in_specs=[vmem] * 3,
        out_specs=(hbm,) * 3,
        scratch_shapes=[dma((3,))],
        compiler_params=pltpu.CompilerParams(vmem_limit_bytes=16 * 1024 * 1024),
    )(*outs)


def solution(mesh):
    return jax.shard_map(
        functools.partial(shards, mesh.shape["wide"], mesh.shape["slab"]),
        mesh=mesh,
        in_specs=(
            P("wide", "slab", None, None),
            P("wide", "slab", None, None),
            P(None, "wide", "slab", None, None),
            P("wide", "slab"),
            P("wide", "slab"),
            P("wide", "slab", None),
            P("wide", "slab", None),
        ),
        out_specs=(P("wide", "slab", None, None), P("wide", "slab"), P("wide", "slab", None)),
        check_vma=False,
    )
```
